32 devices in a mesh: fg: 4 (over y, core), sp: 8 (over z, x).
Axes of the slice: x: 2, y: 2, z: 4, core: 2. Of those that a mesh axis runs over, the one named last changes fastest.
Arguments:
- latent: bfloat16 [16, 64, 240, 256], P('fg', 'sp'), may hold values from -6 to 6
- temporal_weight: bfloat16 [3, 256, 1024], replicated, may hold values from -0.21875 to 0.21875
- temporal_bias: float32 [1024], replicated, may hold values from -4 to 4
- spatial_weight: bfloat16 [3, 3, 256, 128], replicated, may hold values from -0.125 to 0.125
- spatial_bias: float32 [128], replicated, may hold values from -4 to 4
- counts: int32 [4], replicated, may hold values from 1 to 16, 48 in all
Outputs:
- decoded: bfloat16 [64, 64, 240, 128], P('fg', 'sp')
The draws below stay inside these ranges and needn't reach their ends.
Inputs may be any that keep to these rules, and one draw needn't show every extreme that they name: `counts`: some group holds 16.
All inputs are finite; a program needn't handle non-finite values.
Results may differ from the reference program's by a relative error of at most 0.0038.
Values may be sent and summed in bfloat16 or wider, within the bound.
A program may use at most 320 MiB of HBM per device.

```python
import math
import jax
import jax.numpy as jnp
import numpy as np
from jax import lax

CT = 256
CS = 128
W = 240
LF = 4
LATENT = 16
FRAMES = 64
H = 64
N_FG = 4


def block_scale(key, dims, cuts, least, largest):
    def one(axis_at, parts):
        heights = jax.random.uniform(jax.random.fold_in(jax.random.fold_in(key, 6), axis_at), (parts,), jnp.float32, least / len(cuts), largest / len(cuts))
        return jnp.repeat(jnp.exp(heights), dims[axis_at] // parts).reshape((-1,) + (1,) * (len(dims) - axis_at - 1))

    gain = one(*cuts[0])
    for cut in cuts[1:]:
        gain = gain * one(*cut)
    return gain


def split_up(amount, total, limit, lean):
    portions = [(1 << 20) // math.isqrt(standing ** lean) + 1 for standing in range(2, amount + 1)]
    rest, given = total - limit - (amount - 1), [1] * (amount - 1)
    while rest > 0:
        free = [i for i in range(amount - 1) if given[i] < limit]
        pool, budget = sum([portions[i] for i in free]), rest
        for i in free:
            more = min(limit - given[i], max(1, budget * portions[i] // pool), rest)
            given[i] = given[i] + more
            rest = rest - more
    return np.array([limit] + given)


def ragged(key, number_of, total, limit, lean):
    if number_of == 2:
        one = jax.random.randint(key, (), max(1, total - limit), min(limit, total - 1) + 1)
        return jnp.stack([one, total - one])
    tallies = jnp.asarray(split_up(number_of, total, limit, lean), jnp.int32)
    twos = (number_of - 1) // 2
    source_of, sink = tallies[1:1 + 2 * twos:2], tallies[2:2 + 2 * twos:2]
    room = jnp.minimum(source_of - 1, limit - sink)
    shifted = jax.random.randint(jax.random.fold_in(key, 1), (twos,), 0, 1 << 20) % (room + 1)
    tallies = tallies.at[1:1 + 2 * twos:2].set(source_of - shifted).at[2:2 + 2 * twos:2].set(sink + shifted)
    return tallies[jax.random.permutation(jax.random.fold_in(key, 2), number_of)]


def bell_draw(key, shape, width, most, shards=(), held_as=jnp.bfloat16):
    values = width * jax.random.normal(key, shape, jnp.float32)
    if shards:
        values = values * block_scale(key, shape, shards, -0.22, 0.18)
    return jnp.clip(values, -most, most).astype(held_as)


def setup_inputs(seed: int = 0) -> dict:
    arg_keys = jax.random.split(jax.random.key(seed), 7)
    return {
        "latent": bell_draw(arg_keys[0], (LATENT, H, W, CT), 1.0, 6.0, ((0, 4), (1, 8))),
        "temporal_weight": bell_draw(arg_keys[1], (3, CT, 4 * CT), (3 * CT) ** -0.5, 0.21875),
        "temporal_bias": bell_draw(arg_keys[2], (4 * CT,), 1.0, 4.0, (), jnp.float32),
        "spatial_weight": bell_draw(arg_keys[3], (3, 3, CT, CS), (9 * CT) ** -0.5, 0.125),
        "spatial_bias": bell_draw(arg_keys[4], (CS,), 1.0, 4.0, (), jnp.float32),
        "counts": ragged(arg_keys[5], N_FG, 3 * LF * N_FG, 4 * LF, 1).astype(jnp.int32),
    }


def reference(latent, temporal_weight, temporal_bias, spatial_weight, spatial_bias, counts):
    zeros = jnp.zeros((2,) + latent.shape[1:], jnp.bfloat16)
    padded = jnp.concatenate([zeros, latent], axis=0)
    kernel = temporal_weight.astype(jnp.float32).reshape(3, CT, 4, CT)
    bias_t = temporal_bias.reshape(4, 1, 1, CT)
    swf = spatial_weight.astype(jnp.float32)

    def one_frame(index):
        window = lax.dynamic_slice_in_dim(padded, index, 3, 0).astype(jnp.float32)
        pre = jnp.einsum("khwc,kcjd->jhwd", window, kernel) + bias_t
        upper = jax.nn.silu(pre).astype(jnp.bfloat16)
        framed = jnp.pad(upper, ((0, 0), (1, 1), (1, 1), (0, 0))).astype(jnp.float32)
        total = jnp.zeros((4, H, W, CS), jnp.float32)
        for dy in range(3):
            for dx in range(3):
                total = total + jnp.einsum("fhwc,cd->fhwd", framed[:, dy:dy + H, dx:dx + W, :], swf[dy, dx])
        out = (total + spatial_bias).astype(jnp.bfloat16)
        frame_ids = 4 * index + jnp.arange(4, dtype=jnp.int32)
        group = frame_ids // (4 * LF)
        valid = (frame_ids % (4 * LF)) < counts[group]
        return out * valid.astype(jnp.bfloat16).reshape(4, 1, 1, 1)

    result = lax.map(one_frame, jnp.arange(LATENT, dtype=jnp.int32))
    return result.reshape(FRAMES, H, W, CS)
```

```python
import functools

import jax
import jax.numpy as jnp
from jax import lax
from jax.experimental import pallas as pl
from jax.experimental.pallas import tpu as pltpu
from jax.sharding import PartitionSpec as P

F32, BF16 = jnp.float32, jnp.bfloat16
LIMIT = 58 * 1024 * 1024
MESH = pl.DeviceIdType.MESH
SENDS = ((0, 1), (0, -1), (1, 1), (1, -1), (1, 0))
NEIGHBOURS = tuple((f, s) for f in (-1, 0, 1) for s in (-1, 0, 1) if f or s)


def silu(pre):
    half = 0.5 * pre
    return half + half * jnp.tanh(half)


def fill_weights(sw_ref, w01, w2):
    depth, wide = sw_ref.shape[2], sw_ref.shape[3]
    zero = jnp.zeros((depth, wide), BF16)
    for dy in range(3):
        at = pl.ds(dy * depth, depth)
        w01[at, :wide] = sw_ref[dy, 0]
        w01[at, wide:] = sw_ref[dy, 1]
    for q in range(4):
        at = pl.ds(q * depth, depth)
        w2[at, :wide] = sw_ref[q, 2] if q < 3 else zero
        w2[at, wide:] = sw_ref[q - 1, 2] if q > 0 else zero


def activation(a, j, tw_ref, tb_ref):
    width = tw_ref.shape[1] // 4
    columns = pl.ds(pl.multiple_of(j * width, width), width)
    pre = jnp.dot(a, tw_ref[:, columns], preferred_element_type=F32) + tb_ref[:, columns]
    return silu(pre).astype(BF16)


def zero_rims(left, right, cols):
    n, _, wide = left.shape
    left[:, 0:8, :] = jnp.zeros((n, 8, wide), F32)
    right[:, cols:cols + 8, :] = jnp.zeros((n, 8, wide), F32)


def row_pair(row, cols, w01, w2, left, right, sb_ref, p):
    wide = sb_ref.shape[1]
    taps = [row(q) for q in range(4)]
    a = jnp.concatenate([jnp.concatenate(taps[h:h + 3], axis=1) for h in range(2)], axis=0)
    r = jnp.dot(a, w01[...], preferred_element_type=F32)
    s = jnp.dot(jnp.concatenate(taps, axis=1), w2[...], preferred_element_type=F32)
    rows = []
    for h in range(2):
        left[2 * p + h, 8:8 + cols, :] = r[h * cols:(h + 1) * cols, :wide]
        right[2 * p + h, 0:cols, :] = s[:, h * wide:(h + 1) * wide]
        middle = r[h * cols:(h + 1) * cols, wide:] + sb_ref[...]
        rows.append((left[2 * p + h, 7:7 + cols, :] + middle + right[2 * p + h, 1:1 + cols, :]).astype(BF16))
    return rows


def late_kernel(sizes, latent_ref, tw_ref, tb_ref, sw_ref, sb_ref, out_ref, halo_ref, edge_ref,
                lat, up, w01, w2, w3, left, right, load_sem, send_sem, recv_sem):
    frames, rows, cols, width = latent_ref.shape
    wide = sb_ref.shape[1]
    fg, sp = lax.axis_index("fg"), lax.axis_index("sp")

    loads = [pltpu.make_async_copy(latent_ref.at[f], lat.at[f], load_sem.at[f]) for f in range(frames)]
    for load in loads:
        load.start()

    def there(by, back=False):
        f, s = (fg - by[0], sp - by[1]) if back else (fg + by[0], sp + by[1])
        return (f >= 0) & (f < sizes[0]) & (s >= 0) & (s < sizes[1])

    barrier = pltpu.get_barrier_semaphore()
    for by in NEIGHBOURS:
        @pl.when(there(by))
        def _():
            pl.semaphore_signal(barrier, inc=1, device_id=(fg + by[0], sp + by[1]), device_id_type=MESH)
    near = [1 + (at > 0).astype(jnp.int32) + (at < n - 1).astype(jnp.int32) for at, n in zip((fg, sp), sizes)]
    pl.semaphore_wait(barrier, near[0] * near[1] - 1)

    last, head = latent_ref.at[:, rows - 1], latent_ref.at[:, 0]
    tail = pl.ds(frames - 2, 2)
    sources = (last, head, latent_ref.at[tail, rows - 1], latent_ref.at[tail, 0], latent_ref.at[tail])
    own, corner = pl.ds(2, frames), pl.ds(0, 2)
    targets = (halo_ref.at[0, own], halo_ref.at[1, own], halo_ref.at[0, corner], halo_ref.at[1, corner], edge_ref)

    def sent(i):
        by = SENDS[i]
        return pltpu.make_async_remote_copy(
            src_ref=sources[i], dst_ref=targets[i], send_sem=send_sem.at[i], recv_sem=recv_sem.at[i],
            device_id=(fg + by[0], sp + by[1]), device_id_type=MESH,
        )

    for i, by in enumerate(SENDS):
        @pl.when(there(by))
        def _():
            sent(i).start()

    fill_weights(sw_ref, w01, w2)
    for dy in range(3):
        for dx in range(3):
            w3[dy * width:(dy + 1) * width, dx * wide:(dx + 1) * wide] = sw_ref[dy, dx]
    zero_rims(left, right, cols)
    for load in loads:
        load.wait()

    def inner(i, carry):
        l, j = i // 4, i % 4
        a = jnp.concatenate([lat[l + k].reshape(rows * cols, width) for k in range(3)], axis=1)
        up[i] = activation(a, j, tw_ref, tb_ref)
        for p in range(rows // 2 - 1):
            row = lambda q: up[i, pl.ds((2 * p + q) * cols, cols), :]
            for h, value in enumerate(row_pair(row, cols, w01, w2, left, right, sb_ref, p)):
                out_ref[i, 2 * p + 1 + h] = value
        return carry

    lax.fori_loop(0, 8, inner, 0)

    for i in range(2):
        @pl.when(there(SENDS[i], True))
        def _():
            sent(i).wait_recv()

    def rim(i, carry):
        l, j = i // 4, i % 4
        a = jnp.concatenate([halo_ref[:, 2 + l + k].reshape(2 * cols, width) for k in range(3)], axis=1)
        act = activation(a, j, tw_ref, tb_ref)
        zero = jnp.zeros((cols, width), BF16)
        row = lambda h: up[i, pl.ds(h * cols, cols), :]
        above = [jnp.where(sp > 0, act[:cols], zero), row(0), row(1)]
        below = [row(rows - 2), row(rows - 1), jnp.where(sp < sizes[1] - 1, act[cols:], zero)]
        a = jnp.concatenate([jnp.concatenate(above, axis=1), jnp.concatenate(below, axis=1)], axis=0)
        r = jnp.dot(a, w3[...], preferred_element_type=F32)
        for h in range(2):
            part = r[h * cols:(h + 1) * cols]
            left[h, 8:8 + cols, :] = part[:, :wide]
            right[h, 0:cols, :] = part[:, 2 * wide:]
            total = left[h, 7:7 + cols, :] + (part[:, wide:2 * wide] + sb_ref[...]) + right[h, 1:1 + cols, :]
            out_ref[i, h * (rows - 1)] = total.astype(BF16)
        return carry

    lax.fori_loop(0, 8, rim, 0)

    for i, by in enumerate(SENDS):
        if i >= 2:
            @pl.when(there(by, True))
            def _():
                sent(i).wait_recv()

        @pl.when(there(by))
        def _():
            sent(i).wait_send()


def late_call(sizes, latent, tw, tb, sw, sb):
    frames, rows, cols, width = latent.shape
    wide = sw.shape[3]
    vmem = pl.BlockSpec(memory_space=pltpu.VMEM)
    hbm = pl.BlockSpec(memory_space=pl.ANY)
    return pl.pallas_call(
        functools.partial(late_kernel, sizes),
        in_specs=[hbm] + [vmem] * 4,
        out_specs=[vmem, vmem, hbm],
        out_shape=[
            jax.ShapeDtypeStruct((8, rows, cols, wide), BF16),
            jax.ShapeDtypeStruct((2, frames + 2, cols, width), BF16),
            jax.ShapeDtypeStruct((2, rows, cols, width), BF16),
        ],
        scratch_shapes=[
            pltpu.VMEM((frames, rows, cols, width), BF16),
            pltpu.VMEM((8, rows * cols, width), BF16),
            pltpu.VMEM((3 * width, 2 * wide), BF16),
            pltpu.VMEM((4 * width, 2 * wide), BF16),
            pltpu.VMEM((3 * width, 3 * wide), BF16),
            pltpu.VMEM((rows, cols + 8, wide), F32),
            pltpu.VMEM((rows, cols + 8, wide), F32),
            pltpu.SemaphoreType.DMA((frames,)),
            pltpu.SemaphoreType.DMA((len(SENDS),)),
            pltpu.SemaphoreType.DMA((len(SENDS),)),
        ],
        compiler_params=pltpu.CompilerParams(
            collective_id=0, has_side_effects=True, vmem_limit_bytes=LIMIT
        ),
        cost_estimate=pl.CostEstimate(flops=18 * 10**9, bytes_accessed=16 * 10**6, transcendentals=5 * 10**6),
        name="late_frames",
    )(latent, tw, tb, sw, sb)


def early_kernel(counts_ref, edge_ref, latent_ref, halo_ref, late_ref, tw_ref, tb_ref, sw_ref, sb_ref, out_ref,
                 x_ref, up, w01, w2, left, right):
    rows, cols, width = latent_ref.shape[1:]
    fg, sp = lax.axis_index("fg"), lax.axis_index("sp")
    last_sp = lax.axis_size("sp") - 1
    l, j = pl.program_id(0), pl.program_id(1)
    step = 4 * l + j

    @pl.when(step == 0)
    def _():
        fill_weights(sw_ref, w01, w2)
        zero_rims(left, right, cols)

    def put(k, at, frame):
        x_ref[at * cols:at * cols + frame.shape[0], k * width:(k + 1) * width] = frame

    for at in range(2):
        @pl.when((l == at) & (j == 0))
        def _():
            for k in range(3):
                source = at + k - 2
                top, bottom = halo_ref[0, source + 2], halo_ref[1, source + 2]
                if source < 0:
                    body = edge_ref[source + 2].reshape(rows * cols, width)
                    top, body, bottom = (jnp.where(fg > 0, a, jnp.zeros_like(a)) for a in (top, body, bottom))
                else:
                    body = latent_ref[source].reshape(rows * cols, width)
                put(k, 0, top)
                put(k, 1, body)
                put(k, rows + 1, bottom)

    limit = counts_ref[fg]
    valid = step < limit

    @pl.when(valid)
    def _():
        up[...] = activation(x_ref[...], j, tw_ref, tb_ref)

        @pl.when(sp == 0)
        def _():
            up[0:cols, :] = jnp.zeros((cols, width), BF16)

        @pl.when(sp == last_sp)
        def _():
            up[(rows + 1) * cols:, :] = jnp.zeros((cols, width), BF16)

        for p in range(rows // 2):
            row = lambda q: up[pl.ds((2 * p + q) * cols, cols), :]
            for h, value in enumerate(row_pair(row, cols, w01, w2, left, right, sb_ref, p)):
                out_ref[0, 0, 2 * p + h] = value

    @pl.when(jnp.logical_not(valid))
    def _():
        out_ref[0] = jnp.zeros(out_ref.shape[1:], BF16)

    @pl.when(step + 8 < limit)
    def _():
        out_ref[1] = late_ref[...]

    @pl.when(step + 8 >= limit)
    def _():
        out_ref[1] = jnp.zeros(out_ref.shape[1:], BF16)


def early_call(counts, edge, latent, halo, late, tw, tb, sw, sb):
    frames, rows, cols, width = latent.shape
    wide = sw.shape[3]
    whole = lambda a: pl.BlockSpec(a.shape, lambda l, j: (0,) * a.ndim)
    out = pl.pallas_call(
        early_kernel,
        grid=(2, 4),
        in_specs=[
            pl.BlockSpec(memory_space=pltpu.SMEM),
            whole(edge),
            pl.BlockSpec((2, rows, cols, width), lambda l, j: (0, 0, 0, 0)),
            whole(halo),
            pl.BlockSpec((1, rows, cols, wide), lambda l, j: (4 * l + j, 0, 0, 0)),
        ]
        + [whole(a) for a in (tw, tb, sw, sb)],
        out_specs=pl.BlockSpec((2, 1, rows, cols, wide), lambda l, j: (0, 4 * l + j, 0, 0, 0)),
        out_shape=jax.ShapeDtypeStruct((2, 8, rows, cols, wide), BF16),
        scratch_shapes=[
            pltpu.VMEM(((rows + 2) * cols, 3 * width), BF16),
            pltpu.VMEM(((rows + 2) * cols, width), BF16),
            pltpu.VMEM((3 * width, 2 * wide), BF16),
            pltpu.VMEM((4 * width, 2 * wide), BF16),
            pltpu.VMEM((rows, cols + 8, wide), F32),
            pltpu.VMEM((rows, cols + 8, wide), F32),
        ],
        compiler_params=pltpu.CompilerParams(
            dimension_semantics=("arbitrary", "arbitrary"), vmem_limit_bytes=LIMIT
        ),
        cost_estimate=pl.CostEstimate(flops=18 * 10**9, bytes_accessed=20 * 10**6, transcendentals=5 * 10**6),
        name="early_frames",
    )(counts, edge, latent, halo, late, tw, tb, sw, sb)
    return out.reshape(16, rows, cols, wide)


def on_device(sizes, latent, temporal_weight, temporal_bias, spatial_weight, spatial_bias, counts):
    width = latent.shape[3]
    tw = temporal_weight.reshape(3 * width, 4 * width)
    args = (tw, temporal_bias.reshape(1, -1), spatial_weight, spatial_bias.reshape(1, -1))
    late, halo, edge = late_call(sizes, latent, *args)
    return early_call(counts, edge, latent, halo, late, *args)


def solution(mesh):
    sizes = (mesh.shape["fg"], mesh.shape["sp"])
    return jax.shard_map(
        functools.partial(on_device, sizes),
        mesh=mesh,
        in_specs=(P("fg", "sp", None, None), P(), P(), P(), P(), P()),
        out_specs=P("fg", "sp", None, None),
        check_vma=False,
    )
```

```python
import functools

import jax
import jax.numpy as jnp
from jax import lax
from jax.experimental import pallas as pl
from jax.experimental.pallas import tpu as pltpu
from jax.sharding import PartitionSpec as P

F32, BF16 = jnp.float32, jnp.bfloat16
LIMIT = 58 * 1024 * 1024
MESH = pl.DeviceIdType.MESH
SENDS = ((0, 1), (0, -1), (1, 1), (1, -1), (1, 0))
NEIGHBOURS = tuple((f, s) for f in (-1, 0, 1) for s in (-1, 0, 1) if f or s)


def silu(pre):
    half = 0.5 * pre
    return half + half * jnp.tanh(half)


def fill_weights(sw_ref, w01, w2):
    depth, wide = sw_ref.shape[2], sw_ref.shape[3]
    zero = jnp.zeros((depth, wide), BF16)
    for dy in range(3):
        at = pl.ds(dy * depth, depth)
        w01[at, :wide] = sw_ref[dy, 0]
        w01[at, wide:] = sw_ref[dy, 1]
    for q in range(4):
        at = pl.ds(q * depth, depth)
        w2[at, :wide] = sw_ref[q, 2] if q < 3 else zero
        w2[at, wide:] = sw_ref[q - 1, 2] if q > 0 else zero


def activation(a, j, tw_ref, tb_ref):
    width = tw_ref.shape[1] // 4
    columns = pl.ds(pl.multiple_of(j * width, width), width)
    pre = jnp.dot(a, tw_ref[:, columns], preferred_element_type=F32) + tb_ref[:, columns]
    return silu(pre).astype(BF16)


def zero_rims(left, right, cols):
    n, _, wide = left.shape
    left[:, 0:8, :] = jnp.zeros((n, 8, wide), F32)
    right[:, cols:cols + 8, :] = jnp.zeros((n, 8, wide), F32)


def row_pair(row, cols, w01, w2, left, mid, right, sb_ref, p):
    wide = sb_ref.shape[1]
    taps = [row(q) for q in range(4)]
    a = jnp.concatenate([jnp.concatenate(taps[h:h + 3], axis=1) for h in range(2)], axis=0)
    r = jnp.dot(a, w01[...], preferred_element_type=F32)
    s = jnp.dot(jnp.concatenate(taps, axis=1), w2[...], preferred_element_type=F32)
    rows = []
    for h in range(2):
        left[2 * p + h, 8:8 + cols, :] = r[h * cols:(h + 1) * cols, :wide]
        right[2 * p + h, 0:cols, :] = s[:, h * wide:(h + 1) * wide]
        mid[2 * p + h] = r[h * cols:(h + 1) * cols, wide:]
        total = left[2 * p + h, 7:7 + cols, :] + mid[2 * p + h] + right[2 * p + h, 1:1 + cols, :] + sb_ref[...]
        rows.append(total.astype(BF16))
    return rows


def late_kernel(sizes, latent_ref, tw_ref, tb_ref, sw_ref, sb_ref, out_ref, halo_ref, edge_ref,
                lat, up, w01, w2, w3, left, mid, right, load_sem, send_sem, recv_sem):
    frames, rows, cols, width = latent_ref.shape
    wide = sb_ref.shape[1]
    fg, sp = lax.axis_index("fg"), lax.axis_index("sp")

    loads = [pltpu.make_async_copy(latent_ref.at[f], lat.at[f], load_sem.at[f]) for f in range(frames)]
    for load in loads:
        load.start()

    def there(by, back=False):
        f, s = (fg - by[0], sp - by[1]) if back else (fg + by[0], sp + by[1])
        return (f >= 0) & (f < sizes[0]) & (s >= 0) & (s < sizes[1])

    barrier = pltpu.get_barrier_semaphore()
    for by in NEIGHBOURS:
        @pl.when(there(by))
        def _():
            pl.semaphore_signal(barrier, inc=1, device_id=(fg + by[0], sp + by[1]), device_id_type=MESH)
    near = [1 + (at > 0).astype(jnp.int32) + (at < n - 1).astype(jnp.int32) for at, n in zip((fg, sp), sizes)]
    pl.semaphore_wait(barrier, near[0] * near[1] - 1)

    last, head = latent_ref.at[:, rows - 1], latent_ref.at[:, 0]
    tail = pl.ds(frames - 2, 2)
    sources = (last, head, latent_ref.at[tail, rows - 1], latent_ref.at[tail, 0], latent_ref.at[tail])
    own, corner = pl.ds(2, frames), pl.ds(0, 2)
    targets = (halo_ref.at[0, own], halo_ref.at[1, own], halo_ref.at[0, corner], halo_ref.at[1, corner], edge_ref)

    def sent(i):
        by = SENDS[i]
        return pltpu.make_async_remote_copy(
            src_ref=sources[i], dst_ref=targets[i], send_sem=send_sem.at[i], recv_sem=recv_sem.at[i],
            device_id=(fg + by[0], sp + by[1]), device_id_type=MESH,
        )

    for i, by in enumerate(SENDS):
        @pl.when(there(by))
        def _():
            sent(i).start()

    fill_weights(sw_ref, w01, w2)
    for dy in range(3):
        for dx in range(3):
            w3[dy * width:(dy + 1) * width, dx * wide:(dx + 1) * wide] = sw_ref[dy, dx]
    zero_rims(left, right, cols)
    for load in loads:
        load.wait()

    def inner(i, carry):
        l, j = i // 4, i % 4
        for t in range(0, rows, 2):
            a = jnp.concatenate([lat[l + k, t:t + 2].reshape(2 * cols, width) for k in range(3)], axis=1)
            up[i, t * cols:(t + 2) * cols, :] = activation(a, j, tw_ref, tb_ref)
        for p in range(rows // 2 - 1):
            row = lambda q: up[i, pl.ds((2 * p + q) * cols, cols), :]
            for h, value in enumerate(row_pair(row, cols, w01, w2, left, mid, right, sb_ref, p)):
                out_ref[i, 2 * p + 1 + h] = value
        return carry

    lax.fori_loop(0, 8, inner, 0)

    for i in range(2):
        @pl.when(there(SENDS[i], True))
        def _():
            sent(i).wait_recv()

    def rim(i, carry):
        l, j = i // 4, i % 4
        a = jnp.concatenate([halo_ref[:, 2 + l + k].reshape(2 * cols, width) for k in range(3)], axis=1)
        act = activation(a, j, tw_ref, tb_ref)
        zero = jnp.zeros((cols, width), BF16)
        row = lambda h: up[i, pl.ds(h * cols, cols), :]
        above = [jnp.where(sp > 0, act[:cols], zero), row(0), row(1)]
        below = [row(rows - 2), row(rows - 1), jnp.where(sp < sizes[1] - 1, act[cols:], zero)]
        a = jnp.concatenate([jnp.concatenate(above, axis=1), jnp.concatenate(below, axis=1)], axis=0)
        r = jnp.dot(a, w3[...], preferred_element_type=F32)
        for h in range(2):
            part = r[h * cols:(h + 1) * cols]
            left[h, 8:8 + cols, :] = part[:, :wide]
            right[h, 0:cols, :] = part[:, 2 * wide:]
            total = left[h, 7:7 + cols, :] + (part[:, wide:2 * wide] + sb_ref[...]) + right[h, 1:1 + cols, :]
            out_ref[i, h * (rows - 1)] = total.astype(BF16)
        return carry

    lax.fori_loop(0, 8, rim, 0)

    for i, by in enumerate(SENDS):
        if i >= 2:
            @pl.when(there(by, True))
            def _():
                sent(i).wait_recv()

        @pl.when(there(by))
        def _():
            sent(i).wait_send()


def late_call(sizes, latent, tw, tb, sw, sb):
    frames, rows, cols, width = latent.shape
    wide = sw.shape[3]
    vmem = pl.BlockSpec(memory_space=pltpu.VMEM)
    hbm = pl.BlockSpec(memory_space=pl.ANY)
    return pl.pallas_call(
        functools.partial(late_kernel, sizes),
        in_specs=[hbm] + [vmem] * 4,
        out_specs=[vmem, vmem, hbm],
        out_shape=[
            jax.ShapeDtypeStruct((8, rows, cols, wide), BF16),
            jax.ShapeDtypeStruct((2, frames + 2, cols, width), BF16),
            jax.ShapeDtypeStruct((2, rows, cols, width), BF16),
        ],
        scratch_shapes=[
            pltpu.VMEM((frames, rows, cols, width), BF16),
            pltpu.VMEM((8, rows * cols, width), BF16),
            pltpu.VMEM((3 * width, 2 * wide), BF16),
            pltpu.VMEM((4 * width, 2 * wide), BF16),
            pltpu.VMEM((3 * width, 3 * wide), BF16),
            pltpu.VMEM((rows, cols + 8, wide), F32),
            pltpu.VMEM((rows, cols, wide), F32),
            pltpu.VMEM((rows, cols + 8, wide), F32),
            pltpu.SemaphoreType.DMA((frames,)),
            pltpu.SemaphoreType.DMA((len(SENDS),)),
            pltpu.SemaphoreType.DMA((len(SENDS),)),
        ],
        compiler_params=pltpu.CompilerParams(
            collective_id=0, has_side_effects=True, vmem_limit_bytes=LIMIT
        ),
        cost_estimate=pl.CostEstimate(flops=18 * 10**9, bytes_accessed=16 * 10**6, transcendentals=5 * 10**6),
        name="late_frames",
    )(latent, tw, tb, sw, sb)


def early_kernel(counts_ref, edge_ref, latent_ref, halo_ref, late_ref, tw_ref, tb_ref, sw_ref, sb_ref, out_ref,
                 x_ref, up, w01, w2, left, mid, right):
    rows, cols, width = latent_ref.shape[1:]
    fg, sp = lax.axis_index("fg"), lax.axis_index("sp")
    last_sp = lax.axis_size("sp") - 1
    l, j = pl.program_id(0), pl.program_id(1)
    step = 4 * l + j

    @pl.when(step == 0)
    def _():
        fill_weights(sw_ref, w01, w2)
        zero_rims(left, right, cols)

    def put(k, at, frame):
        x_ref[at * cols:at * cols + frame.shape[0], k * width:(k + 1) * width] = frame

    for at in range(2):
        @pl.when((l == at) & (j == 0))
        def _():
            for k in range(3):
                source = at + k - 2
                top, bottom = halo_ref[0, source + 2], halo_ref[1, source + 2]
                if source < 0:
                    body = edge_ref[source + 2].reshape(rows * cols, width)
                    top, body, bottom = (jnp.where(fg > 0, a, jnp.zeros_like(a)) for a in (top, body, bottom))
                else:
                    body = latent_ref[source].reshape(rows * cols, width)
                put(k, 0, top)
                put(k, 1, body)
                put(k, rows + 1, bottom)

    limit = counts_ref[fg]
    valid = step < limit

    @pl.when(valid)
    def _():
        for t in range(0, rows + 2, 2):
            at = pl.ds(t * cols, 2 * cols)
            up[at, :] = activation(x_ref[at, :], j, tw_ref, tb_ref)

        @pl.when(sp == 0)
        def _():
            up[0:cols, :] = jnp.zeros((cols, width), BF16)

        @pl.when(sp == last_sp)
        def _():
            up[(rows + 1) * cols:, :] = jnp.zeros((cols, width), BF16)

        for p in range(rows // 2):
            row = lambda q: up[pl.ds((2 * p + q) * cols, cols), :]
            for h, value in enumerate(row_pair(row, cols, w01, w2, left, mid, right, sb_ref, p)):
                out_ref[0, 0, 2 * p + h] = value

    @pl.when(jnp.logical_not(valid))
    def _():
        out_ref[0] = jnp.zeros(out_ref.shape[1:], BF16)

    @pl.when(step + 8 < limit)
    def _():
        out_ref[1] = late_ref[...]

    @pl.when(step + 8 >= limit)
    def _():
        out_ref[1] = jnp.zeros(out_ref.shape[1:], BF16)


def early_call(counts, edge, latent, halo, late, tw, tb, sw, sb):
    frames, rows, cols, width = latent.shape
    wide = sw.shape[3]
    whole = lambda a: pl.BlockSpec(a.shape, lambda l, j: (0,) * a.ndim)
    out = pl.pallas_call(
        early_kernel,
        grid=(2, 4),
        in_specs=[
            pl.BlockSpec(memory_space=pltpu.SMEM),
            whole(edge),
            pl.BlockSpec((2, rows, cols, width), lambda l, j: (0, 0, 0, 0)),
            whole(halo),
            pl.BlockSpec((1, rows, cols, wide), lambda l, j: (4 * l + j, 0, 0, 0)),
        ]
        + [whole(a) for a in (tw, tb, sw, sb)],
        out_specs=pl.BlockSpec((2, 1, rows, cols, wide), lambda l, j: (0, 4 * l + j, 0, 0, 0)),
        out_shape=jax.ShapeDtypeStruct((2, 8, rows, cols, wide), BF16),
        scratch_shapes=[
            pltpu.VMEM(((rows + 2) * cols, 3 * width), BF16),
            pltpu.VMEM(((rows + 2) * cols, width), BF16),
            pltpu.VMEM((3 * width, 2 * wide), BF16),
            pltpu.VMEM((4 * width, 2 * wide), BF16),
            pltpu.VMEM((rows, cols + 8, wide), F32),
            pltpu.VMEM((rows, cols, wide), F32),
            pltpu.VMEM((rows, cols + 8, wide), F32),
        ],
        compiler_params=pltpu.CompilerParams(
            dimension_semantics=("arbitrary", "arbitrary"), vmem_limit_bytes=LIMIT
        ),
        cost_estimate=pl.CostEstimate(flops=18 * 10**9, bytes_accessed=20 * 10**6, transcendentals=5 * 10**6),
        name="early_frames",
    )(counts, edge, latent, halo, late, tw, tb, sw, sb)
    return out.reshape(16, rows, cols, wide)


def on_device(sizes, latent, temporal_weight, temporal_bias, spatial_weight, spatial_bias, counts):
    width = latent.shape[3]
    tw = temporal_weight.reshape(3 * width, 4 * width)
    args = (tw, temporal_bias.reshape(1, -1), spatial_weight, spatial_bias.reshape(1, -1))
    late, halo, edge = late_call(sizes, latent, *args)
    return early_call(counts, edge, latent, halo, late, *args)


def solution(mesh):
    sizes = (mesh.shape["fg"], mesh.shape["sp"])
    return jax.shard_map(
        functools.partial(on_device, sizes),
        mesh=mesh,
        in_specs=(P("fg", "sp", None, None), P(), P(), P(), P(), P()),
        out_specs=P("fg", "sp", None, None),
        check_vma=False,
    )
```

```python
import functools

import jax
import jax.numpy as jnp
from jax import lax
from jax.experimental import pallas as pl
from jax.experimental.pallas import tpu as pltpu
from jax.sharding import PartitionSpec as P

F32, BF16 = jnp.float32, jnp.bfloat16
LIMIT = 58 * 1024 * 1024
MESH = pl.DeviceIdType.MESH
SENDS = ((0, 1), (0, -1), (1, 1), (1, -1), (1, 0))
NEIGHBOURS = tuple((f, s) for f in (-1, 0, 1) for s in (-1, 0, 1) if f or s)


def silu(pre):
    half = 0.5 * pre
    return half + half * jnp.tanh(half)


def fill_weights(sw_ref, w01, w2):
    depth, wide = sw_ref.shape[2], sw_ref.shape[3]
    zero = jnp.zeros((depth, wide), BF16)
    for dy in range(3):
        at = pl.ds(dy * depth, depth)
        w01[at, :wide] = sw_ref[dy, 0]
        w01[at, wide:] = sw_ref[dy, 1]
    for q in range(4):
        at = pl.ds(q * depth, depth)
        w2[at, :wide] = sw_ref[q, 2] if q < 3 else zero
        w2[at, wide:] = sw_ref[q - 1, 2] if q > 0 else zero


def activation(a, j, tw_ref, tb_ref):
    width = tw_ref.shape[1] // 4
    columns = pl.ds(pl.multiple_of(j * width, width), width)
    pre = jnp.dot(a, tw_ref[:, columns], preferred_element_type=F32) + tb_ref[:, columns]
    return silu(pre).astype(BF16)


def zero_rims(left, right, cols):
    n, _, wide = left.shape
    left[:, 0:8, :] = jnp.zeros((n, 8, wide), F32)
    right[:, cols:cols + 8, :] = jnp.zeros((n, 8, wide), F32)


def row_pair(row, cols, w01, w2, left, mid, right, sb_ref, p):
    wide = sb_ref.shape[1]
    taps = [row(q) for q in range(4)]
    a = jnp.concatenate([jnp.concatenate(taps[h:h + 3], axis=1) for h in range(2)], axis=0)
    r = jnp.dot(a, w01[...], preferred_element_type=F32)
    s = jnp.dot(jnp.concatenate(taps, axis=1), w2[...], preferred_element_type=F32)
    rows = []
    for h in range(2):
        left[2 * p + h, 8:8 + cols, :] = r[h * cols:(h + 1) * cols, :wide]
        right[2 * p + h, 0:cols, :] = s[:, h * wide:(h + 1) * wide]
        mid[2 * p + h] = r[h * cols:(h + 1) * cols, wide:]
        total = left[2 * p + h, 7:7 + cols, :] + mid[2 * p + h] + right[2 * p + h, 1:1 + cols, :] + sb_ref[...]
        rows.append(total.astype(BF16))
    return rows


def late_kernel(sizes, latent_ref, tw_ref, tb_ref, sw_ref, sb_ref, out_ref, halo_ref, edge_ref,
                lat, up, w01, w2, w3, left, mid, right, load_sem, send_sem, recv_sem):
    frames, rows, cols, width = latent_ref.shape
    wide = sb_ref.shape[1]
    fg, sp = lax.axis_index("fg"), lax.axis_index("sp")

    loads = [pltpu.make_async_copy(latent_ref.at[f], lat.at[f], load_sem.at[f]) for f in range(frames)]
    for load in loads:
        load.start()

    def there(by, back=False):
        f, s = (fg - by[0], sp - by[1]) if back else (fg + by[0], sp + by[1])
        return (f >= 0) & (f < sizes[0]) & (s >= 0) & (s < sizes[1])

    barrier = pltpu.get_barrier_semaphore()
    for by in NEIGHBOURS:
        @pl.when(there(by))
        def _():
            pl.semaphore_signal(barrier, inc=1, device_id=(fg + by[0], sp + by[1]), device_id_type=MESH)
    near = [1 + (at > 0).astype(jnp.int32) + (at < n - 1).astype(jnp.int32) for at, n in zip((fg, sp), sizes)]
    pl.semaphore_wait(barrier, near[0] * near[1] - 1)

    last, head = latent_ref.at[:, rows - 1], latent_ref.at[:, 0]
    tail = pl.ds(frames - 2, 2)
    sources = (last, head, latent_ref.at[tail, rows - 1], latent_ref.at[tail, 0], latent_ref.at[tail])
    own, corner = pl.ds(2, frames), pl.ds(0, 2)
    targets = (halo_ref.at[0, own], halo_ref.at[1, own], halo_ref.at[0, corner], halo_ref.at[1, corner], edge_ref)

    def sent(i):
        by = SENDS[i]
        return pltpu.make_async_remote_copy(
            src_ref=sources[i], dst_ref=targets[i], send_sem=send_sem.at[i], recv_sem=recv_sem.at[i],
            device_id=(fg + by[0], sp + by[1]), device_id_type=MESH,
        )

    for i in (4, 0, 1, 2, 3):
        @pl.when(there(SENDS[i]))
        def _():
            sent(i).start()

    fill_weights(sw_ref, w01, w2)
    for dy in range(3):
        for dx in range(3):
            w3[dy * width:(dy + 1) * width, dx * wide:(dx + 1) * wide] = sw_ref[dy, dx]
    zero_rims(left, right, cols)
    for load in loads:
        load.wait()

    def inner(i, carry):
        l, j = i // 4, i % 4
        for t in range(0, rows, 2):
            a = jnp.concatenate([lat[l + k, t:t + 2].reshape(2 * cols, width) for k in range(3)], axis=1)
            up[i, t * cols:(t + 2) * cols, :] = activation(a, j, tw_ref, tb_ref)
        for p in range(rows // 2 - 1):
            row = lambda q: up[i, pl.ds((2 * p + q) * cols, cols), :]
            for h, value in enumerate(row_pair(row, cols, w01, w2, left, mid, right, sb_ref, p)):
                out_ref[i, 2 * p + 1 + h] = value
        return carry

    lax.fori_loop(0, 8, inner, 0)

    for i in range(2):
        @pl.when(there(SENDS[i], True))
        def _():
            sent(i).wait_recv()

    def rim(i, carry):
        l, j = i // 4, i % 4
        a = jnp.concatenate([halo_ref[:, 2 + l + k].reshape(2 * cols, width) for k in range(3)], axis=1)
        act = activation(a, j, tw_ref, tb_ref)
        zero = jnp.zeros((cols, width), BF16)
        row = lambda h: up[i, pl.ds(h * cols, cols), :]
        above = [jnp.where(sp > 0, act[:cols], zero), row(0), row(1)]
        below = [row(rows - 2), row(rows - 1), jnp.where(sp < sizes[1] - 1, act[cols:], zero)]
        a = jnp.concatenate([jnp.concatenate(above, axis=1), jnp.concatenate(below, axis=1)], axis=0)
        r = jnp.dot(a, w3[...], preferred_element_type=F32)
        for h in range(2):
            part = r[h * cols:(h + 1) * cols]
            left[h, 8:8 + cols, :] = part[:, :wide]
            right[h, 0:cols, :] = part[:, 2 * wide:]
            total = left[h, 7:7 + cols, :] + (part[:, wide:2 * wide] + sb_ref[...]) + right[h, 1:1 + cols, :]
            out_ref[i, h * (rows - 1)] = total.astype(BF16)
        return carry

    lax.fori_loop(0, 8, rim, 0)

    for i, by in enumerate(SENDS):
        if i >= 2:
            @pl.when(there(by, True))
            def _():
                sent(i).wait_recv()

        @pl.when(there(by))
        def _():
            sent(i).wait_send()


def late_call(sizes, latent, tw, tb, sw, sb):
    frames, rows, cols, width = latent.shape
    wide = sw.shape[3]
    vmem = pl.BlockSpec(memory_space=pltpu.VMEM)
    hbm = pl.BlockSpec(memory_space=pl.ANY)
    return pl.pallas_call(
        functools.partial(late_kernel, sizes),
        in_specs=[hbm] + [vmem] * 4,
        out_specs=[vmem, vmem, hbm],
        out_shape=[
            jax.ShapeDtypeStruct((8, rows, cols, wide), BF16),
            jax.ShapeDtypeStruct((2, frames + 2, cols, width), BF16),
            jax.ShapeDtypeStruct((2, rows, cols, width), BF16),
        ],
        scratch_shapes=[
            pltpu.VMEM((frames, rows, cols, width), BF16),
            pltpu.VMEM((8, rows * cols, width), BF16),
            pltpu.VMEM((3 * width, 2 * wide), BF16),
            pltpu.VMEM((4 * width, 2 * wide), BF16),
            pltpu.VMEM((3 * width, 3 * wide), BF16),
            pltpu.VMEM((rows, cols + 8, wide), F32),
            pltpu.VMEM((rows, cols, wide), F32),
            pltpu.VMEM((rows, cols + 8, wide), F32),
            pltpu.SemaphoreType.DMA((frames,)),
            pltpu.SemaphoreType.DMA((len(SENDS),)),
            pltpu.SemaphoreType.DMA((len(SENDS),)),
        ],
        compiler_params=pltpu.CompilerParams(
            collective_id=0, has_side_effects=True, vmem_limit_bytes=LIMIT
        ),
        cost_estimate=pl.CostEstimate(flops=18 * 10**9, bytes_accessed=16 * 10**6, transcendentals=5 * 10**6),
        name="late_frames",
    )(latent, tw, tb, sw, sb)


def early_kernel(counts_ref, edge_ref, latent_ref, halo_ref, late_ref, tw_ref, tb_ref, sw_ref, sb_ref, out_ref,
                 x_ref, up, w01, w2, left, mid, right):
    rows, cols, width = latent_ref.shape[1:]
    fg, sp = lax.axis_index("fg"), lax.axis_index("sp")
    last_sp = lax.axis_size("sp") - 1
    l, j = pl.program_id(0), pl.program_id(1)
    step = 4 * l + j

    @pl.when(step == 0)
    def _():
        fill_weights(sw_ref, w01, w2)
        zero_rims(left, right, cols)

    def put(k, at, frame):
        x_ref[at * cols:at * cols + frame.shape[0], k * width:(k + 1) * width] = frame

    for at in range(2):
        @pl.when((l == at) & (j == 0))
        def _():
            for k in range(3):
                source = at + k - 2
                top, bottom = halo_ref[0, source + 2], halo_ref[1, source + 2]
                if source < 0:
                    body = edge_ref[source + 2].reshape(rows * cols, width)
                    top, body, bottom = (jnp.where(fg > 0, a, jnp.zeros_like(a)) for a in (top, body, bottom))
                else:
                    body = latent_ref[source].reshape(rows * cols, width)
                put(k, 0, top)
                put(k, 1, body)
                put(k, rows + 1, bottom)

    limit = counts_ref[fg]
    valid = step < limit

    @pl.when(valid)
    def _():
        for t in range(0, rows + 2, 2):
            at = pl.ds(t * cols, 2 * cols)
            up[at, :] = activation(x_ref[at, :], j, tw_ref, tb_ref)

        @pl.when(sp == 0)
        def _():
            up[0:cols, :] = jnp.zeros((cols, width), BF16)

        @pl.when(sp == last_sp)
        def _():
            up[(rows + 1) * cols:, :] = jnp.zeros((cols, width), BF16)

        for p in range(rows // 2):
            row = lambda q: up[pl.ds((2 * p + q) * cols, cols), :]
            for h, value in enumerate(row_pair(row, cols, w01, w2, left, mid, right, sb_ref, p)):
                out_ref[0, 0, 2 * p + h] = value

    @pl.when(jnp.logical_not(valid))
    def _():
        out_ref[0] = jnp.zeros(out_ref.shape[1:], BF16)

    @pl.when(step + 8 < limit)
    def _():
        out_ref[1] = late_ref[...]

    @pl.when(step + 8 >= limit)
    def _():
        out_ref[1] = jnp.zeros(out_ref.shape[1:], BF16)


def early_call(counts, edge, latent, halo, late, tw, tb, sw, sb):
    frames, rows, cols, width = latent.shape
    wide = sw.shape[3]
    whole = lambda a: pl.BlockSpec(a.shape, lambda l, j: (0,) * a.ndim)
    out = pl.pallas_call(
        early_kernel,
        grid=(2, 4),
        in_specs=[
            pl.BlockSpec(memory_space=pltpu.SMEM),
            whole(edge),
            pl.BlockSpec((2, rows, cols, width), lambda l, j: (0, 0, 0, 0)),
            whole(halo),
            pl.BlockSpec((1, rows, cols, wide), lambda l, j: (4 * l + j, 0, 0, 0)),
        ]
        + [whole(a) for a in (tw, tb, sw, sb)],
        out_specs=pl.BlockSpec((2, 1, rows, cols, wide), lambda l, j: (0, 4 * l + j, 0, 0, 0)),
        out_shape=jax.ShapeDtypeStruct((2, 8, rows, cols, wide), BF16),
        scratch_shapes=[
            pltpu.VMEM(((rows + 2) * cols, 3 * width), BF16),
            pltpu.VMEM(((rows + 2) * cols, width), BF16),
            pltpu.VMEM((3 * width, 2 * wide), BF16),
            pltpu.VMEM((4 * width, 2 * wide), BF16),
            pltpu.VMEM((rows, cols + 8, wide), F32),
            pltpu.VMEM((rows, cols, wide), F32),
            pltpu.VMEM((rows, cols + 8, wide), F32),
        ],
        compiler_params=pltpu.CompilerParams(
            dimension_semantics=("arbitrary", "arbitrary"), vmem_limit_bytes=LIMIT
        ),
        cost_estimate=pl.CostEstimate(flops=18 * 10**9, bytes_accessed=20 * 10**6, transcendentals=5 * 10**6),
        name="early_frames",
    )(counts, edge, latent, halo, late, tw, tb, sw, sb)
    return out.reshape(16, rows, cols, wide)


def on_device(sizes, latent, temporal_weight, temporal_bias, spatial_weight, spatial_bias, counts):
    width = latent.shape[3]
    tw = temporal_weight.reshape(3 * width, 4 * width)
    args = (tw, temporal_bias.reshape(1, -1), spatial_weight, spatial_bias.reshape(1, -1))
    late, halo, edge = late_call(sizes, latent, *args)
    return early_call(counts, edge, latent, halo, late, *args)


def solution(mesh):
    sizes = (mesh.shape["fg"], mesh.shape["sp"])
    return jax.shard_map(
        functools.partial(on_device, sizes),
        mesh=mesh,
        in_specs=(P("fg", "sp", None, None), P(), P(), P(), P(), P()),
        out_specs=P("fg", "sp", None, None),
        check_vma=False,
    )
```
